512 devices in a mesh: depth: 32 (over z_lo, y, core), row: 16 (over z_hi, x).
Axes of the slice: x: 4, y: 8, z: 8 (z_hi: 4, z_lo: 2; z = z_hi * 2 + z_lo), core: 2. Of those that a mesh axis runs over, the one named last changes fastest.
Arguments:
- input_cells: bfloat16 [128, 256, 128, 128], P('depth', 'row'), may hold values from -6 to 6
- first_weight: bfloat16 [3, 3, 3, 64, 128], P(None, None, None, None, 'depth'), may hold values from -0.15625 to 0.15625
- second_weight: bfloat16 [3, 3, 3, 128, 256], P(None, None, None, None, 'depth'), may hold values from -0.109375 to 0.109375
Outputs:
- encoded: bfloat16 [32, 64, 32, 512], P('depth', 'row')
The draws below stay inside these ranges and needn't reach their ends.
All inputs are finite; a program needn't handle non-finite values.
Results may differ from the reference program's by a relative error of at most 0.0049.
Values may be sent and summed in bfloat16 or wider, within the bound.
No kernel may reach another device: no remote copies, remote signals or barrier semaphores. Data moves between devices by JAX's collectives and lax.ppermute only.
A program may use at most 64 MiB of HBM per device.

```python
import math
import jax
import jax.numpy as jnp
from jax import lax

IN_CH = 64
MID_CH = 128
OUT_CH = 256
CELLS_W = 256
DEPTH = 128
ROWS = 256


def block_scale(rng, dims, split, smallest, largest):
    loudness, own = 1.0, jax.random.fold_in(rng, 6)
    for dim, shards_of in split:
        heights = jnp.exp(jax.random.uniform(jax.random.fold_in(own, dim), (shards_of,), jnp.float32, smallest / len(split), largest / len(split)))
        loudness = loudness * jnp.repeat(heights, dims[dim] // shards_of).reshape([-1 if axis == dim else 1 for axis in range(len(dims))])
    return loudness


def centred(stream_key, shape, deviation, bound, pieces=(), kind=jnp.bfloat16):
    result = jax.random.normal(stream_key, shape, jnp.float32) * deviation
    if len(pieces) > 0:
        result = block_scale(stream_key, shape, pieces, -0.22, 0.18) * result
    return jnp.clip(result, min=-bound, max=bound).astype(kind)


def setup_inputs(seed: int = 0) -> dict:
    key_of = jax.random.split(jax.random.key(seed), 4)
    return {
        "input_cells": centred(key_of[0], (DEPTH, ROWS, CELLS_W // 2, 2 * IN_CH), 1.0, 6.0, ((0, 32), (1, 16))),
        "first_weight": centred(key_of[1], (3, 3, 3, IN_CH, MID_CH), (27 * IN_CH) ** -0.5, 0.15625, ((4, 32),)),
        "second_weight": centred(key_of[2], (3, 3, 3, MID_CH, OUT_CH), (27 * MID_CH) ** -0.5, 0.109375, ((4, 32),)),
    }


def stacked(weight, depth_tap, row_tap):
    kernel_taps = weight[depth_tap, row_tap]
    zeros_block = jnp.zeros_like(kernel_taps[0])
    upper_part = jnp.concatenate([kernel_taps[1], kernel_taps[2]], 0)
    lower_part = jnp.concatenate([zeros_block, kernel_taps[0]], 0)
    return jnp.concatenate([upper_part, lower_part], 1)


def convolve(extended, weight):
    planes = extended.shape[0] - 1
    row_count = extended.shape[1] - 1
    pair_count = extended.shape[2]
    features = extended.shape[3]
    out_width = weight.shape[4]
    running = jnp.zeros(((planes // 2) * (row_count // 2) * pair_count, 2 * out_width), jnp.float32)
    for depth_tap in range(3):
        for row_tap in range(3):
            window = extended[depth_tap:depth_tap + planes:2, row_tap:row_tap + row_count:2]
            running = running + jnp.dot(window.reshape(-1, features), stacked(weight, depth_tap, row_tap), preferred_element_type=jnp.float32)
    running = running.reshape(planes // 2, row_count // 2, pair_count, 2 * out_width)
    carried = jnp.pad(running[:, :, :-1, out_width:], ((0, 0), (0, 0), (1, 0), (0, 0)))
    return running[..., :out_width] + carried


def finish(field):
    activated = jnp.maximum(field, 0.0).astype(jnp.bfloat16)
    shape_now = activated.shape
    return activated.reshape(shape_now[0], shape_now[1], shape_now[2] // 2, 2 * shape_now[3])


def layer(field, weight):
    extended = jnp.pad(field, ((1, 0), (1, 0), (0, 0), (0, 0)))
    planes = field.shape[0]
    block = math.gcd(planes // 2, 8)
    block_count = planes // 2 // block

    def one_block(block_index):
        slab_cells = lax.dynamic_slice_in_dim(extended, (block_index * 2 * block).astype(jnp.int32), 2 * block + 1, 0)
        return finish(convolve(slab_cells, weight))

    blocks = lax.map(one_block, jnp.arange(block_count, dtype=jnp.int32))
    return blocks.reshape((planes // 2,) + blocks.shape[2:])


def reference(input_cells, first_weight, second_weight):
    hidden = layer(input_cells, first_weight)
    return layer(hidden, second_weight)
```

```python
import jax
import jax.numpy as jnp
from jax import lax
from jax.experimental import pallas as pl
from jax.experimental.pallas import tpu as pltpu
from jax.sharding import PartitionSpec as P

F32 = jnp.float32
BF16 = jnp.bfloat16
VMEM = pltpu.VMEM
SPEC = pl.BlockSpec(memory_space=pltpu.VMEM)


def dot_t(a, b):
    return lax.dot_general(a, b, (((1,), (1,)), ((), ())), preferred_element_type=F32)


def first_kernel(x_ref, plane_ref, rim_ref, corner_ref, g_ref, h0_ref, h1_ref, stage, rows_up, weights, up, low):
    lanes = lax.broadcasted_iota(jnp.int32, (128, 128), 1)
    right = lanes >= 64
    for tile in range(7):
        stage[...] = g_ref[tile // 4, :, tile % 4].astype(F32).reshape(256, 128)
        for r in range(8):
            rows_up[r // 4, pl.ds(r % 4, 32, stride=4)] = stage[pl.ds(r, 32, stride=8)]
        for half in range(2):
            group = 2 * tile + half
            block = rows_up[half]
            if group < 9:
                weights[group, 0:128] = block.astype(BF16)
            else:
                tap = 2 * (group - 9)
                weights[tap, 128:256] = jnp.where(right, pltpu.roll(block, 64, 1), 0.0).astype(BF16)
                if tap + 1 < 9:
                    weights[tap + 1, 128:256] = jnp.where(right, block, 0.0).astype(BF16)

    def window(plane, j):
        if plane == 0:
            x, rim = plane_ref[0], corner_ref[0]
        else:
            x, rim = x_ref[plane - 1], rim_ref[plane - 1]
        x = x.reshape(8, 2, 128, 128)
        if j == 0:
            parts = [rim[0:1], rim[2:3], x[0:7, 1]]
        elif j == 1:
            parts = [rim[1:2], x[:, 0]]
        else:
            parts = [rim[2:3], x[:, 1]]
        return jnp.concatenate(parts, 0).reshape(1152, 128)

    for a in range(2):
        for tap in range(9):
            i, j = divmod(tap, 3)
            both = dot_t(window(2 * a + i, j), weights[tap]).reshape(9, 128, 256)
            if tap == 0:
                up[...] = both[:, :, :128]
                low[:, 8:136] = both[:, :, 128:]
                low[:, 0:8] = jnp.zeros((9, 8, 128), F32)
            else:
                up[...] += both[:, :, :128]
                low[:, 8:136] += both[:, :, 128:]
        out = (h0_ref, h1_ref)[a]
        for b in range(9):
            even = up[b, pl.ds(0, 64, stride=2)] + low[b, pl.ds(7, 64, stride=2)]
            odd = up[b, pl.ds(1, 64, stride=2)] + low[b, pl.ds(8, 64, stride=2)]
            out[b, :, 0:128] = jnp.maximum(even, 0.0).astype(BF16)
            out[b, :, 128:256] = jnp.maximum(odd, 0.0).astype(BF16)


def first_layer(x, plane, rim, corner, g):
    shape = jax.ShapeDtypeStruct((9, 64, 256), BF16)
    return pl.pallas_call(
        first_kernel,
        out_shape=(shape, shape),
        in_specs=[SPEC] * 5,
        out_specs=(SPEC, SPEC),
        scratch_shapes=[
            VMEM((256, 128), F32),
            VMEM((2, 128, 128), F32),
            VMEM((9, 256, 128), BF16),
            VMEM((9, 128, 128), F32),
            VMEM((9, 136, 128), F32),
        ],
        compiler_params=pltpu.CompilerParams(vmem_limit_bytes=40 * 2**20),
        cost_estimate=pl.CostEstimate(flops=2 * 2304 * 1152 * 256, bytes_accessed=4 * 2**20, transcendentals=0),
        name="first_layer",
    )(x, plane, rim, corner, g)


def second_kernel(core_ref, hm_ref, h0_ref, h1_ref, g_ref, mine_ref, theirs_ref, out_ref, up, low):
    planes = (hm_ref, h0_ref, h1_ref)

    def weight(block):
        return block.astype(F32).reshape(256, 128).astype(BF16)

    def body(first_ref, last_ref):
        low[:, :, 0:8] = jnp.zeros((2, 4, 8, 128), F32)

        def tap_of(t):
            if t < 13:
                return weight(first_ref[:, t])
            if t == 13:
                return weight(g_ref[1, :, 3])
            return weight(last_ref[:, t - 14])

        for tap in range(9):
            i, j = divmod(tap, 3)
            cells = jnp.concatenate([planes[i][j + 2 * b] for b in range(4)], 0)
            k0, k1, k2 = (tap_of(3 * tap + k) for k in range(3))
            u = dot_t(cells, jnp.concatenate([k1, k2], 1))
            v = dot_t(cells[:, 128:], k0).reshape(4, 64, 256)
            for n in range(2):
                lanes = slice(128 * n, 128 * n + 128)
                if tap == 0:
                    up[n] = u[:, lanes]
                    low[n, :, 8:72] = v[:, :, lanes]
                else:
                    up[n] += u[:, lanes]
                    low[n, :, 8:72] += v[:, :, lanes]

    @pl.when(core_ref[0] == 0)
    def _():
        body(mine_ref, theirs_ref)

    @pl.when(core_ref[0] != 0)
    def _():
        body(theirs_ref, mine_ref)

    for b in range(4):
        for n in range(2):
            even = up[n, pl.ds(64 * b, 32, stride=2)] + low[n, b, pl.ds(7, 32, stride=2)]
            odd = up[n, pl.ds(64 * b + 1, 32, stride=2)] + low[n, b, pl.ds(8, 32, stride=2)]
            out_ref[0, b, :, 128 * n : 128 * n + 128] = jnp.maximum(even, 0.0).astype(BF16)
            out_ref[0, b, :, 256 + 128 * n : 384 + 128 * n] = jnp.maximum(odd, 0.0).astype(BF16)


def second_layer(core, hm, h0, h1, g, mine, theirs):
    return pl.pallas_call(
        second_kernel,
        out_shape=jax.ShapeDtypeStruct((1, 4, 32, 512), BF16),
        in_specs=[pl.BlockSpec(memory_space=pltpu.SMEM)] + [SPEC] * 6,
        out_specs=SPEC,
        scratch_shapes=[VMEM((2, 256, 128), F32), VMEM((2, 4, 72, 128), F32)],
        compiler_params=pltpu.CompilerParams(vmem_limit_bytes=40 * 2**20),
        cost_estimate=pl.CostEstimate(flops=2 * 256 * 3456 * 256, bytes_accessed=3 * 2**20, transcendentals=0),
        name="second_layer",
    )(core, hm, h0, h1, g, mine, theirs)


def packed(first, second):
    taps = first.transpose(0, 1, 2, 4, 3).reshape(9, 3, 4, 64)
    pair = jnp.concatenate([taps[:, 1], taps[:, 2]], -1)
    single = jnp.pad(taps[:, 0], ((0, 1), (0, 0), (0, 0))).reshape(5, 2, 4, 64)
    single = jnp.concatenate([single[:, 0], single[:, 1]], -1)
    w1 = jnp.concatenate([pair, single], 0).reshape(7, 8, 128)
    w2 = second.transpose(0, 1, 2, 4, 3).reshape(27, 8, 128)
    half0 = jnp.concatenate([w1[:4], w2[:13]], 0)
    half1 = jnp.concatenate([w1[4:], w2[13:]], 0)
    return jnp.stack([half0, half1])


def shift_by_one(x, axes, counts):
    if len(axes) == 1:
        pairs = [(i, i + 1) for i in range(counts[0] - 1)]
        return lax.ppermute(x, axes[0], pairs)
    n, m = counts
    pairs = [(i * m + j, (i + 1) * m + j + 1) for i in range(n - 1) for j in range(m - 1)]
    return lax.ppermute(x, axes, pairs)


def per_device(x, first_weight, second_weight):
    nd, nr = lax.axis_size("depth"), lax.axis_size("row")
    halves = packed(first_weight, second_weight)
    send = jnp.broadcast_to(halves[None], (nd // 2, 2, 17, 8, 128)).reshape(nd, 17, 8, 128)
    got = lax.all_to_all(send, "depth", 0, 0, tiled=False)

    rim = shift_by_one(x[:, 13:], ("row",), (nr,))
    plane = shift_by_one(x[3:], ("depth",), (nd,))
    corner = shift_by_one(x[3:, 13:], ("depth", "row"), (nd, nr))

    got, rim, plane, corner = lax.optimization_barrier((got, rim, plane, corner))

    partners = [(i, i ^ 1) for i in range(nd)]
    groups = [[i, i + 1] for i in range(0, nd, 2)]
    g = lax.all_gather(got[:, :4], "depth", axis_index_groups=groups)
    mine = got[:, 4:]
    theirs = lax.ppermute(mine, "depth", partners)

    h0, h1 = first_layer(x, plane, rim, corner, g)
    hm = shift_by_one(h1, ("depth",), (nd,))
    core = (lax.axis_index("depth") % 2).astype(jnp.int32).reshape(1)
    return second_layer(core, hm, h0, h1, g, mine, theirs)


def solution(mesh):
    return jax.shard_map(
        per_device,
        mesh=mesh,
        in_specs=(
            P("depth", "row", None, None),
            P(None, None, None, None, "depth"),
            P(None, None, None, None, "depth"),
        ),
        out_specs=P("depth", "row", None, None),
        check_vma=False,
    )
```

```python
import jax
import jax.numpy as jnp
from jax import lax
from jax.experimental import pallas as pl
from jax.experimental.pallas import tpu as pltpu
from jax.sharding import PartitionSpec as P

F32 = jnp.float32
BF16 = jnp.bfloat16
VMEM = pltpu.VMEM
SPEC = pl.BlockSpec(memory_space=pltpu.VMEM)


def dot_t(a, b):
    return lax.dot_general(a, b, (((1,), (1,)), ((), ())), preferred_element_type=F32)


def first_kernel(x_ref, edge_ref, rim_ref, mine_ref, theirs_ref, seen_ref, h0_ref, h1_ref, rows_ref, stage, rows_up, weights, up, low):
    lanes = lax.broadcasted_iota(jnp.int32, (128, 128), 1)
    right = lanes >= 64
    core = lax.axis_index("depth") & 1

    def unpack(lower_ref, upper_ref):
        for tile in range(7):
            stage[...] = (lower_ref, upper_ref)[tile // 4][:, tile % 4].astype(F32).reshape(256, 128)
            for r in range(8):
                rows_up[r // 4, pl.ds(r % 4, 32, stride=4)] = stage[pl.ds(r, 32, stride=8)]
            for half in range(2):
                group = 2 * tile + half
                block = rows_up[half]
                if group < 9:
                    weights[group, 0:128] = block.astype(BF16)
                else:
                    tap = 2 * (group - 9)
                    weights[tap, 128:256] = jnp.where(right, pltpu.roll(block, 64, 1), 0.0).astype(BF16)
                    if tap + 1 < 9:
                        weights[tap + 1, 128:256] = jnp.where(right, block, 0.0).astype(BF16)

    @pl.when(core == 0)
    def _():
        unpack(mine_ref, theirs_ref)

    @pl.when(core != 0)
    def _():
        unpack(theirs_ref, mine_ref)

    def window(plane, j):
        x = edge_ref[0] if plane == 0 else x_ref[plane - 1]
        x = x.reshape(8, 2, 128, 128)
        if j == 0:
            x = jnp.concatenate([rim_ref[plane], x[0:7, 1]], 0)
        else:
            x = x[:, j - 1]
        return x.reshape(1024, 128)

    for a in range(2):
        for tap in range(9):
            i, j = divmod(tap, 3)
            both = dot_t(window(2 * a + i, j), weights[tap]).reshape(8, 128, 256)
            if tap == 0:
                up[...] = both[:, :, :128]
                low[:, 8:136] = both[:, :, 128:]
                low[:, 0:8] = jnp.zeros((8, 8, 128), F32)
            else:
                up[...] += both[:, :, :128]
                low[:, 8:136] += both[:, :, 128:]
        out = (h0_ref, h1_ref)[a]
        for b in range(8):
            even = up[b, pl.ds(0, 64, stride=2)] + low[b, pl.ds(7, 64, stride=2)]
            odd = up[b, pl.ds(1, 64, stride=2)] + low[b, pl.ds(8, 64, stride=2)]
            out[b, :, 0:128] = jnp.maximum(even, 0.0).astype(BF16)
            out[b, :, 128:256] = jnp.maximum(odd, 0.0).astype(BF16)
        rows_ref[a] = out[7]


def first_layer(x, edge, rim, mine, theirs, seen):
    shape = jax.ShapeDtypeStruct((8, 64, 256), BF16)
    rows = jax.ShapeDtypeStruct((2, 64, 256), BF16)
    return pl.pallas_call(
        first_kernel,
        out_shape=(shape, shape, rows),
        in_specs=[SPEC] * 6,
        out_specs=(SPEC, SPEC, SPEC),
        scratch_shapes=[
            VMEM((256, 128), F32),
            VMEM((2, 128, 128), F32),
            VMEM((9, 256, 128), BF16),
            VMEM((8, 128, 128), F32),
            VMEM((8, 136, 128), F32),
        ],
        compiler_params=pltpu.CompilerParams(vmem_limit_bytes=24 * 2**20),
        cost_estimate=pl.CostEstimate(flops=2 * 2048 * 1152 * 256, bytes_accessed=4 * 2**20, transcendentals=0),
        name="first_layer",
    )(x, edge, rim, mine, theirs, seen)


def second_kernel(hm_ref, h0_ref, h1_ref, rows_ref, mine_ref, theirs_ref, stripe_ref, other_ref, out_ref, up, low):
    core, odd = lax.axis_index("depth") & 1, lax.axis_index("row") & 1

    def row(plane, at):
        if plane == 0:
            return hm_ref[at]
        return rows_ref[plane - 1] if at == 0 else (h0_ref, h1_ref)[plane - 1][at - 1]

    def weight(block):
        return block.astype(F32).reshape(256, 128).astype(BF16)

    def body(first, last, odd):
        low[:, :, 0:8] = jnp.zeros((2, 4, 8, 128), F32)

        def tap_of(t):
            if t == 13:
                return weight(last[0][:, 3])
            own, across = first if t < 13 else last
            place = t if t < 13 else t - 14
            if place == 0:
                return weight(own[:, 4])
            side, place = divmod(place - 1, 6)
            return weight(own[:, 5 + place] if side == odd else across[:, place])

        for tap in range(9):
            i, j = divmod(tap, 3)
            cells = jnp.concatenate([row(i, j + 2 * b) for b in range(4)], 0)
            k0, k1, k2 = (tap_of(3 * tap + k) for k in range(3))
            u = dot_t(cells, jnp.concatenate([k1, k2], 1))
            v = dot_t(cells[:, 128:], k0).reshape(4, 64, 256)
            for n in range(2):
                lanes = slice(128 * n, 128 * n + 128)
                if tap == 0:
                    up[n] = u[:, lanes]
                    low[n, :, 8:72] = v[:, :, lanes]
                else:
                    up[n] += u[:, lanes]
                    low[n, :, 8:72] += v[:, :, lanes]

    mine, theirs = (mine_ref, stripe_ref), (theirs_ref, other_ref)
    for c in range(2):
        for q in range(2):

            @pl.when(jnp.logical_and(core == c, odd == q))
            def _():
                body(*((mine, theirs) if c == 0 else (theirs, mine)), q)

    for b in range(4):
        for n in range(2):
            even = up[n, pl.ds(64 * b, 32, stride=2)] + low[n, b, pl.ds(7, 32, stride=2)]
            odd = up[n, pl.ds(64 * b + 1, 32, stride=2)] + low[n, b, pl.ds(8, 32, stride=2)]
            out_ref[0, b, :, 128 * n : 128 * n + 128] = jnp.maximum(even, 0.0).astype(BF16)
            out_ref[0, b, :, 256 + 128 * n : 384 + 128 * n] = jnp.maximum(odd, 0.0).astype(BF16)


def second_layer(hm, h0, h1, rows, mine, theirs, stripe, other):
    return pl.pallas_call(
        second_kernel,
        out_shape=jax.ShapeDtypeStruct((1, 4, 32, 512), BF16),
        in_specs=[SPEC] * 8,
        out_specs=SPEC,
        scratch_shapes=[VMEM((2, 256, 128), F32), VMEM((2, 4, 72, 128), F32)],
        compiler_params=pltpu.CompilerParams(vmem_limit_bytes=24 * 2**20),
        cost_estimate=pl.CostEstimate(flops=2 * 256 * 3456 * 256, bytes_accessed=3 * 2**20, transcendentals=0),
        name="second_layer",
    )(hm, h0, h1, rows, mine, theirs, stripe, other)


def pack_kernel(w1_hbm, w2_hbm, x_ref, send_ref, rim_ref, plane_ref, w1_ref, w2_ref, tiles, sems):
    weights = [
        pltpu.make_async_copy(w1_hbm, w1_ref, sems.at[2]),
        pltpu.make_async_copy(w2_hbm, w2_ref, sems.at[3]),
    ]
    copies = [
        pltpu.make_async_copy(x_ref.at[:, 15:16], rim_ref, sems.at[0]),
        pltpu.make_async_copy(x_ref.at[3:4], plane_ref, sems.at[1]),
    ]
    for copy in weights + copies:
        copy.start()
    odd = lax.axis_index("row") & 1
    for copy in weights:
        copy.wait()

    def tap(k, t):
        return w1_ref[t, k].astype(F32)

    def group(g):
        if g < 9:
            sides = [tap(1, g), tap(2, g)]
        else:
            t = 2 * (g - 9)
            sides = [tap(0, t), tap(0, t + 1) if t < 8 else jnp.zeros((4, 64), F32)]
        return jnp.concatenate(sides, 1)

    for m in range(7):
        tile = jnp.concatenate([group(2 * m), group(2 * m + 1)], 0).astype(BF16)
        tiles[m // 4, m % 4] = tile
    tiles[0, 4] = w2_ref[0]
    tiles[1, 3] = w2_ref[13]
    tiles[1, 4] = w2_ref[14]
    for half in range(2):
        for s in range(6):
            tiles[half, 5 + s] = w2_ref[14 * half + 1 + s + 6 * odd]
    for k in range(send_ref.shape[0] // 2):
        send_ref[2 * k : 2 * k + 2] = tiles[...]
    for copy in copies:
        copy.wait()


def pack(first, second, x, members):
    w1 = first.transpose(0, 1, 2, 4, 3).reshape(9, 3, 4, 64)
    w2 = second.transpose(0, 1, 2, 4, 3).reshape(27, 8, 128)
    shapes = ((members, 11, 8, 128), (4, 1, 128, 128), (1, 16, 128, 128))
    hbm = pl.BlockSpec(memory_space=pltpu.HBM)
    return pl.pallas_call(
        pack_kernel,
        out_shape=tuple(jax.ShapeDtypeStruct(shape, BF16) for shape in shapes),
        in_specs=[hbm, hbm, hbm],
        out_specs=(SPEC, SPEC, SPEC),
        scratch_shapes=[
            VMEM((9, 3, 4, 64), BF16),
            VMEM((27, 8, 128), BF16),
            VMEM((2, 11, 8, 128), BF16),
            pltpu.SemaphoreType.DMA((4,)),
        ],
        compiler_params=pltpu.CompilerParams(vmem_limit_bytes=60 * 2**20),
        name="pack",
    )(w1, w2, x)


def shift_by_one(x, axes, counts):
    if len(axes) == 1:
        pairs = [(i, i + 1) for i in range(counts[0] - 1)]
        return lax.ppermute(x, axes[0], pairs)
    n, m = counts
    pairs = [(i * m + j, (i + 1) * m + j + 1) for i in range(n - 1) for j in range(m - 1)]
    return lax.ppermute(x, axes, pairs)


def per_device(x, first_weight, second_weight):
    nd, nr = lax.axis_size("depth"), lax.axis_size("row")
    send, rim, plane = pack(first_weight, second_weight, x, nd)
    got = lax.all_to_all(send, "depth", 0, 0, tiled=False)

    edge = shift_by_one(plane, ("depth",), (nd,))
    corner = shift_by_one(plane[:, 15:], ("depth", "row"), (nd, nr))
    rim = shift_by_one(rim, ("row",), (nr,))
    rim = jnp.concatenate([corner, rim], 0)
    got, seen = lax.optimization_barrier((got, rim[0, 0, :16] + rim[1, 0, :16] + edge[0, 0, :16]))

    swaps = []
    for i in range(nd):
        for j in range(nr):
            base, at = j - j % 4, j % 4
            other = at ^ 1 if i % 2 == 0 else 3 - at
            swaps.append((i * nr + j, i * nr + base + other))
    stripe = lax.ppermute(got[:, 5:], ("depth", "row"), swaps)

    partners = [(i, i ^ 1) for i in range(nd)]
    theirs = lax.ppermute(got, "depth", partners)
    h0, h1, rows = first_layer(x, edge, rim, got, theirs, seen)
    rows = shift_by_one(rows, ("row",), (nr,))
    h0, stripe = lax.optimization_barrier((h0, stripe))
    hm = shift_by_one(jnp.concatenate([rows[1:], h1], 0), ("depth",), (nd,))
    other = lax.ppermute(stripe, "depth", partners)
    return second_layer(hm, h0, h1, rows, got, theirs, stripe, other)


def solution(mesh):
    return jax.shard_map(
        per_device,
        mesh=mesh,
        in_specs=(
            P("depth", "row", None, None),
            P(None, None, None, None, "depth"),
            P(None, None, None, None, "depth"),
        ),
        out_specs=P("depth", "row", None, None),
        check_vma=False,
    )
```

```python
import jax
import jax.numpy as jnp
from jax import lax
from jax.experimental import pallas as pl
from jax.experimental.pallas import tpu as pltpu
from jax.sharding import PartitionSpec as P

F32 = jnp.float32
BF16 = jnp.bfloat16
VMEM = pltpu.VMEM
SENT = 13
SPEC = pl.BlockSpec(memory_space=pltpu.VMEM)


def dot_t(a, b):
    return lax.dot_general(a, b, (((1,), (1,)), ((), ())), preferred_element_type=F32)


def first_kernel(x_ref, plane_ref, rim_ref, corner_ref, mine_ref, theirs_ref, seen_ref, h0_ref, h1_ref, stage, rows_up, weights, up, low):
    lanes = lax.broadcasted_iota(jnp.int32, (128, 128), 1)
    right = lanes >= 64
    core = lax.axis_index("depth") & 1

    def put(tap, row, block):
        i, j = divmod(tap, 3)
        pair, side = (i, j - 1) if j else (3 + i // 2, i % 2)
        weights[pair, row : row + 128, 128 * side : 128 * side + 128] = block.astype(BF16)

    def unpack(lower_ref, upper_ref):
        for tile in range(7):
            stage[...] = (lower_ref, upper_ref)[tile // 4][:, tile % 4].astype(F32).reshape(256, 128)
            for r in range(8):
                rows_up[r // 4, pl.ds(r % 4, 32, stride=4)] = stage[pl.ds(r, 32, stride=8)]
            for half in range(2):
                group = 2 * tile + half
                block = rows_up[half]
                if group < 9:
                    put(group, 0, block)
                else:
                    tap = 2 * (group - 9)
                    put(tap, 128, jnp.where(right, pltpu.roll(block, 64, 1), 0.0))
                    if tap + 1 < 9:
                        put(tap + 1, 128, jnp.where(right, block, 0.0))

    @pl.when(core == 0)
    def _():
        unpack(mine_ref, theirs_ref)

    @pl.when(core != 0)
    def _():
        unpack(theirs_ref, mine_ref)

    def window(plane, j):
        if plane == 0:
            x, rim = plane_ref[0], corner_ref[0]
        else:
            x, rim = x_ref[plane - 1], rim_ref[plane - 1]
        x = x.reshape(8, 2, 128, 128)
        if j == 0:
            parts = [rim[0:1], rim[2:3], x[0:7, 1]]
        elif j == 1:
            parts = [rim[1:2], x[:, 0]]
        else:
            parts = [rim[2:3], x[:, 1]]
        return jnp.concatenate(parts, 0).reshape(1152, 128)

    h1_ref[9:] = jnp.zeros((SENT - 9, 64, 256), BF16)
    for a in range(2):
        for pair in range(5):
            if pair < 3:
                cells = jnp.concatenate([window(2 * a + pair, 1), window(2 * a + pair, 2)], 1)
            elif pair == 3:
                cells = jnp.concatenate([window(2 * a, 0), window(2 * a + 1, 0)], 1)
            else:
                cells = window(2 * a + 2, 0)
            both = dot_t(cells, weights[pair, :, : cells.shape[1]]).reshape(9, 128, 256)
            if pair == 0:
                up[...] = both[:, :, :128]
                low[:, 8:136] = both[:, :, 128:]
                low[:, 0:8] = jnp.zeros((9, 8, 128), F32)
            else:
                up[...] += both[:, :, :128]
                low[:, 8:136] += both[:, :, 128:]
        out = (h0_ref, h1_ref)[a]
        for b in range(9):
            even = up[b, pl.ds(0, 64, stride=2)] + low[b, pl.ds(7, 64, stride=2)]
            odd = up[b, pl.ds(1, 64, stride=2)] + low[b, pl.ds(8, 64, stride=2)]
            out[b, :, 0:128] = jnp.maximum(even, 0.0).astype(BF16)
            out[b, :, 128:256] = jnp.maximum(odd, 0.0).astype(BF16)


def first_layer(x, plane, rim, corner, mine, theirs, seen):
    h0, h1 = (jax.ShapeDtypeStruct((n, 64, 256), BF16) for n in (9, SENT))
    return pl.pallas_call(
        first_kernel,
        out_shape=(h0, h1),
        in_specs=[SPEC] * 7,
        out_specs=(SPEC, SPEC),
        scratch_shapes=[
            VMEM((256, 128), F32),
            VMEM((2, 128, 128), F32),
            VMEM((5, 256, 256), BF16),
            VMEM((9, 128, 128), F32),
            VMEM((9, 136, 128), F32),
        ],
        compiler_params=pltpu.CompilerParams(vmem_limit_bytes=24 * 2**20),
        cost_estimate=pl.CostEstimate(flops=2 * 2304 * 1152 * 256, bytes_accessed=4 * 2**20, transcendentals=0),
        name="first_layer",
    )(x, plane, rim, corner, mine, theirs, seen)


def second_kernel(hm_ref, h0_ref, h1_ref, mine_ref, theirs_ref, stripe_ref, other_ref, out_ref, up, low):
    core, odd = lax.axis_index("depth") & 1, lax.axis_index("row") & 1
    planes = (hm_ref, h0_ref, h1_ref)

    def weight(block):
        return block.astype(F32).reshape(256, 128).astype(BF16)

    def body(first, last, odd):
        low[:, :, 0:8] = jnp.zeros((2, 4, 8, 128), F32)

        def tap_of(t):
            if t == 13:
                return weight(last[0][:, 3])
            own, across = first if t < 13 else last
            place = t if t < 13 else t - 14
            if place == 0:
                return weight(own[:, 4])
            side, place = divmod(place - 1, 6)
            return weight(own[:, 5 + place] if side == odd else across[:, place])

        for tap in range(9):
            i, j = divmod(tap, 3)
            cells = jnp.concatenate([planes[i][j + 2 * b] for b in range(4)], 0)
            k0, k1, k2 = (tap_of(3 * tap + k) for k in range(3))
            u = dot_t(cells, jnp.concatenate([k1, k2], 1))
            v = dot_t(cells[:, 128:], k0).reshape(4, 64, 256)
            for n in range(2):
                lanes = slice(128 * n, 128 * n + 128)
                if tap == 0:
                    up[n] = u[:, lanes]
                    low[n, :, 8:72] = v[:, :, lanes]
                else:
                    up[n] += u[:, lanes]
                    low[n, :, 8:72] += v[:, :, lanes]

    mine, theirs = (mine_ref, stripe_ref), (theirs_ref, other_ref)
    for c in range(2):
        for q in range(2):

            @pl.when(jnp.logical_and(core == c, odd == q))
            def _():
                body(*((mine, theirs) if c == 0 else (theirs, mine)), q)

    for b in range(4):
        for n in range(2):
            even = up[n, pl.ds(64 * b, 32, stride=2)] + low[n, b, pl.ds(7, 32, stride=2)]
            odd = up[n, pl.ds(64 * b + 1, 32, stride=2)] + low[n, b, pl.ds(8, 32, stride=2)]
            out_ref[0, b, :, 128 * n : 128 * n + 128] = jnp.maximum(even, 0.0).astype(BF16)
            out_ref[0, b, :, 256 + 128 * n : 384 + 128 * n] = jnp.maximum(odd, 0.0).astype(BF16)


def second_layer(hm, h0, h1, mine, theirs, stripe, other):
    return pl.pallas_call(
        second_kernel,
        out_shape=jax.ShapeDtypeStruct((1, 4, 32, 512), BF16),
        in_specs=[SPEC] * 7,
        out_specs=SPEC,
        scratch_shapes=[VMEM((2, 256, 128), F32), VMEM((2, 4, 72, 128), F32)],
        compiler_params=pltpu.CompilerParams(vmem_limit_bytes=24 * 2**20),
        cost_estimate=pl.CostEstimate(flops=2 * 256 * 3456 * 256, bytes_accessed=3 * 2**20, transcendentals=0),
        name="second_layer",
    )(hm, h0, h1, mine, theirs, stripe, other)


def pack_kernel(w1_hbm, w2_hbm, x_ref, send_ref, rim_ref, plane_ref, corner_ref, w1_ref, w2_ref, tiles, sems):
    weights = [
        pltpu.make_async_copy(w1_hbm, w1_ref, sems.at[3]),
        pltpu.make_async_copy(w2_hbm, w2_ref, sems.at[4]),
    ]
    copies = [
        pltpu.make_async_copy(x_ref.at[:, 13:16], rim_ref, sems.at[0]),
        pltpu.make_async_copy(x_ref.at[3:4], plane_ref, sems.at[1]),
        pltpu.make_async_copy(x_ref.at[3:4, 13:16], corner_ref, sems.at[2]),
    ]
    for copy in weights + copies:
        copy.start()
    odd = lax.axis_index("row") & 1
    for copy in weights:
        copy.wait()

    def tap(k, t):
        return w1_ref[t, k].astype(F32)

    def group(g):
        if g < 9:
            sides = [tap(1, g), tap(2, g)]
        else:
            t = 2 * (g - 9)
            sides = [tap(0, t), tap(0, t + 1) if t < 8 else jnp.zeros((4, 64), F32)]
        return jnp.concatenate(sides, 1)

    for m in range(7):
        tile = jnp.concatenate([group(2 * m), group(2 * m + 1)], 0).astype(BF16)
        tiles[m // 4, m % 4] = tile
    tiles[0, 4] = w2_ref[0]
    tiles[1, 3] = w2_ref[13]
    tiles[1, 4] = w2_ref[14]
    for half in range(2):
        for s in range(6):
            tiles[half, 5 + s] = w2_ref[14 * half + 1 + s + 6 * odd]
    for k in range(send_ref.shape[0] // 2):
        send_ref[2 * k : 2 * k + 2] = tiles[...]
    for copy in copies:
        copy.wait()


def pack(first, second, x, members):
    w1 = first.transpose(0, 1, 2, 4, 3).reshape(9, 3, 4, 64)
    w2 = second.transpose(0, 1, 2, 4, 3).reshape(27, 8, 128)
    shapes = ((members, 11, 8, 128), (4, 3, 128, 128), (1, 16, 128, 128), (1, 3, 128, 128))
    hbm = pl.BlockSpec(memory_space=pltpu.HBM)
    return pl.pallas_call(
        pack_kernel,
        out_shape=tuple(jax.ShapeDtypeStruct(shape, BF16) for shape in shapes),
        in_specs=[hbm, hbm, hbm],
        out_specs=(SPEC, SPEC, SPEC, SPEC),
        scratch_shapes=[
            VMEM((9, 3, 4, 64), BF16),
            VMEM((27, 8, 128), BF16),
            VMEM((2, 11, 8, 128), BF16),
            pltpu.SemaphoreType.DMA((5,)),
        ],
        compiler_params=pltpu.CompilerParams(vmem_limit_bytes=60 * 2**20),
        name="pack",
    )(w1, w2, x)


def shift_by_one(x, axes, counts):
    if len(axes) == 1:
        pairs = [(i, i + 1) for i in range(counts[0] - 1)]
        return lax.ppermute(x, axes[0], pairs)
    n, m = counts
    pairs = [(i * m + j, (i + 1) * m + j + 1) for i in range(n - 1) for j in range(m - 1)]
    return lax.ppermute(x, axes, pairs)


def glance_kernel(rim_ref, out_ref):
    out_ref[...] = rim_ref[...]


def glance(rim):
    return pl.pallas_call(
        glance_kernel,
        out_shape=jax.ShapeDtypeStruct((16, 128), BF16),
        in_specs=[SPEC],
        out_specs=SPEC,
        compiler_params=pltpu.CompilerParams(vmem_limit_bytes=2 * 2**20),
        cost_estimate=pl.CostEstimate(flops=10**11, bytes_accessed=2**20, transcendentals=0),
        name="glance",
    )(rim)


def per_device(x, first_weight, second_weight):
    nd, nr = lax.axis_size("depth"), lax.axis_size("row")
    send, rim, plane, corner = pack(first_weight, second_weight, x, nd)
    got = lax.all_to_all(send, "depth", 0, 0, tiled=False)

    rim = shift_by_one(rim, ("row",), (nr,))
    plane = shift_by_one(plane, ("depth",), (nd,))
    corner = shift_by_one(corner, ("depth", "row"), (nd, nr))
    seen = glance(rim[0, 0, :16]) + plane[0, 0, :16] + corner[0, 0, :16]
    got, seen = lax.optimization_barrier((got, seen))

    swaps = []
    for i in range(nd):
        for j in range(nr):
            base, at = j - j % 4, j % 4
            other = at ^ 1 if i % 2 == 0 else 3 - at
            swaps.append((i * nr + j, i * nr + base + other))
    stripe = lax.ppermute(got[:, 5:], ("depth", "row"), swaps)

    partners = [(i, i ^ 1) for i in range(nd)]
    theirs = lax.ppermute(got, "depth", partners)
    h0, h1 = first_layer(x, plane, rim, corner, got, theirs, seen)
    hm = shift_by_one(h1, ("depth",), (nd,))

    h0, stripe = lax.optimization_barrier((h0, stripe))
    other = lax.ppermute(stripe, "depth", partners)
    return second_layer(hm, h0, h1, got, theirs, stripe, other)


def solution(mesh):
    return jax.shard_map(
        per_device,
        mesh=mesh,
        in_specs=(
            P("depth", "row", None, None),
            P(None, None, None, None, "depth"),
            P(None, None, None, None, "depth"),
        ),
        out_specs=P("depth", "row", None, None),
        check_vma=False,
    )
```

```python
import jax
import jax.numpy as jnp
from jax import lax
from jax.experimental import pallas as pl
from jax.experimental.pallas import tpu as pltpu
from jax.sharding import PartitionSpec as P

F32 = jnp.float32
BF16 = jnp.bfloat16
VMEM = pltpu.VMEM
SENT = 13
SPEC = pl.BlockSpec(memory_space=pltpu.VMEM)


def dot_t(a, b):
    return lax.dot_general(a, b, (((1,), (1,)), ((), ())), preferred_element_type=F32)


def window(x, rim, j):
    x = x.reshape(8, 2, 128, 128)
    if j == 0:
        parts = [rim[0:1], rim[2:3], x[0:7, 1]]
    elif j == 1:
        parts = [rim[1:2], x[:, 0]]
    else:
        parts = [rim[2:3], x[:, 1]]
    return jnp.concatenate(parts, 0).reshape(1152, 128)


def plane_of_hidden(cells, weights, out, up, low):
    low[:, 0:8] = jnp.zeros((9, 8, 128), F32)
    for pair in range(5):
        if pair < 3:
            left = jnp.concatenate([cells(pair, 1), cells(pair, 2)], 1)
        elif pair == 3:
            left = jnp.concatenate([cells(0, 0), cells(1, 0)], 1)
        else:
            left = cells(2, 0)
        both = dot_t(left, weights[pair, :, : left.shape[1]]).reshape(9, 128, 256)
        if pair == 0:
            up[:, 0:128] = both[:, :, :128]
            low[:, 8:136] = both[:, :, 128:]
        else:
            up[:, 0:128] += both[:, :, :128]
            low[:, 8:136] += both[:, :, 128:]
    for b in range(9):
        even = up[b, pl.ds(0, 64, stride=2)] + low[b, pl.ds(7, 64, stride=2)]
        odd = up[b, pl.ds(1, 64, stride=2)] + low[b, pl.ds(8, 64, stride=2)]
        out[b, :, 0:128] = jnp.maximum(even, 0.0).astype(BF16)
        out[b, :, 128:256] = jnp.maximum(odd, 0.0).astype(BF16)


def last_kernel(x_ref, plane_hbm, rim_ref, mine_ref, theirs_ref, seen_ref, h1_ref, weights, plane_ref, stage, rows_up, up, low, sem):
    fetch = pltpu.make_async_copy(plane_hbm, plane_ref, sem)
    fetch.start()
    lanes = lax.broadcasted_iota(jnp.int32, (128, 128), 1)
    right = lanes >= 64
    core = lax.axis_index("depth") & 1

    def put(tap, row, block):
        i, j = divmod(tap, 3)
        pair, side = (i, j - 1) if j else (3 + i // 2, i % 2)
        weights[pair, row : row + 128, 128 * side : 128 * side + 128] = block.astype(BF16)

    def unpack(lower_ref, upper_ref):
        for tile in range(7):
            stage[0:256] = (lower_ref, upper_ref)[tile // 4][:, tile % 4].astype(F32).reshape(256, 128)
            for r in range(8):
                rows_up[r // 4, pl.ds(r % 4, 32, stride=4)] = stage[pl.ds(r, 32, stride=8)]
            for half in range(2):
                group = 2 * tile + half
                block = rows_up[half, 0:128]
                if group < 9:
                    put(group, 0, block)
                else:
                    tap = 2 * (group - 9)
                    put(tap, 128, jnp.where(right, pltpu.roll(block, 64, 1), 0.0))
                    if tap + 1 < 9:
                        put(tap + 1, 128, jnp.where(right, block, 0.0))

    @pl.when(core == 0)
    def _():
        unpack(mine_ref, theirs_ref)

    @pl.when(core != 0)
    def _():
        unpack(theirs_ref, mine_ref)

    weights[4, :, 128:256] = jnp.zeros((256, 128), BF16)
    h1_ref[9:] = jnp.zeros((SENT - 9, 64, 256), BF16)

    def cells(i, j):
        return window(x_ref[1 + i], rim_ref[1 + i], j)

    plane_of_hidden(cells, weights, h1_ref, up, low)
    fetch.wait()


def before_kernel(x_ref, plane_ref, rim_ref, corner_ref, weights, h0_ref, up, low):
    def cells(i, j):
        if i == 0:
            return window(plane_ref[0], corner_ref[0], j)
        return window(x_ref[i - 1], rim_ref[i - 1], j)

    plane_of_hidden(cells, weights, h0_ref, up, low)


SUMS = [VMEM((9, 136, 128), F32), VMEM((9, 136, 128), F32)]
HIDDEN = jax.ShapeDtypeStruct((9, 64, 256), BF16)


def last_hidden(x, plane, rim, mine, theirs, seen):
    return pl.pallas_call(
        last_kernel,
        out_shape=(jax.ShapeDtypeStruct((SENT, 64, 256), BF16), jax.ShapeDtypeStruct((5, 256, 256), BF16), jax.ShapeDtypeStruct(plane.shape, BF16)),
        in_specs=[SPEC, pl.BlockSpec(memory_space=pl.ANY)] + [SPEC] * 4,
        out_specs=(SPEC, SPEC, SPEC),
        scratch_shapes=[VMEM((264, 128), F32), VMEM((2, 136, 128), F32)] + SUMS + [pltpu.SemaphoreType.DMA(())],
        compiler_params=pltpu.CompilerParams(vmem_limit_bytes=24 * 2**20),
        cost_estimate=pl.CostEstimate(flops=2 * 1152 * 1152 * 256, bytes_accessed=2 * 2**20, transcendentals=0),
        name="last_hidden",
    )(x, plane, rim, mine, theirs, seen)


def hidden_before(x, plane, rim, corner, weights):
    return pl.pallas_call(
        before_kernel,
        out_shape=HIDDEN,
        in_specs=[SPEC] * 5,
        out_specs=SPEC,
        scratch_shapes=SUMS,
        compiler_params=pltpu.CompilerParams(vmem_limit_bytes=24 * 2**20),
        cost_estimate=pl.CostEstimate(flops=2 * 1152 * 1152 * 256, bytes_accessed=2 * 2**20, transcendentals=0),
        name="hidden_before",
    )(x, plane, rim, corner, weights)


def second_kernel(hm_ref, h0_ref, h1_ref, mine_ref, theirs_ref, stripe_ref, other_ref, out_ref, up, low):
    core, odd = lax.axis_index("depth") & 1, lax.axis_index("row") & 1
    planes = (hm_ref, h0_ref, h1_ref)

    def weight(block):
        return block.astype(F32).reshape(256, 128).astype(BF16)

    def body(first, last, odd):
        low[:, :, 0:8] = jnp.zeros((2, 4, 8, 128), F32)

        def tap_of(t):
            if t == 13:
                return weight(last[0][:, 3])
            own, across = first if t < 13 else last
            place = t if t < 13 else t - 14
            if place == 0:
                return weight(own[:, 4])
            side, place = divmod(place - 1, 6)
            return weight(own[:, 5 + place] if side == odd else across[:, place])

        for tap in range(9):
            i, j = divmod(tap, 3)
            cells = jnp.concatenate([planes[i][j + 2 * b] for b in range(4)], 0)
            k0, k1, k2 = (tap_of(3 * tap + k) for k in range(3))
            u = dot_t(cells, jnp.concatenate([k1, k2], 1))
            v = dot_t(cells[:, 128:], k0).reshape(4, 64, 256)
            for n in range(2):
                lanes = slice(128 * n, 128 * n + 128)
                if tap == 0:
                    up[n, 0:256] = u[:, lanes]
                    low[n, :, 8:72] = v[:, :, lanes]
                else:
                    up[n, 0:256] += u[:, lanes]
                    low[n, :, 8:72] += v[:, :, lanes]

    mine, theirs = (mine_ref, stripe_ref), (theirs_ref, other_ref)
    for c in range(2):
        for q in range(2):

            @pl.when(jnp.logical_and(core == c, odd == q))
            def _():
                body(*((mine, theirs) if c == 0 else (theirs, mine)), q)

    for b in range(4):
        for n in range(2):
            even = up[n, pl.ds(64 * b, 32, stride=2)] + low[n, b, pl.ds(7, 32, stride=2)]
            odd = up[n, pl.ds(64 * b + 1, 32, stride=2)] + low[n, b, pl.ds(8, 32, stride=2)]
            out_ref[0, b, :, 128 * n : 128 * n + 128] = jnp.maximum(even, 0.0).astype(BF16)
            out_ref[0, b, :, 256 + 128 * n : 384 + 128 * n] = jnp.maximum(odd, 0.0).astype(BF16)


def second_layer(hm, h0, h1, mine, theirs, stripe, other):
    return pl.pallas_call(
        second_kernel,
        out_shape=jax.ShapeDtypeStruct((1, 4, 32, 512), BF16),
        in_specs=[SPEC] * 7,
        out_specs=SPEC,
        scratch_shapes=[VMEM((2, 264, 128), F32), VMEM((2, 4, 72, 128), F32)],
        compiler_params=pltpu.CompilerParams(vmem_limit_bytes=24 * 2**20),
        cost_estimate=pl.CostEstimate(flops=2 * 256 * 3456 * 256, bytes_accessed=3 * 2**20, transcendentals=0),
        name="second_layer",
    )(hm, h0, h1, mine, theirs, stripe, other)


def pack_kernel(w1_hbm, w2_hbm, x_ref, send_ref, rim_ref, plane_ref, corner_ref, w1_ref, w2_ref, tiles, sems):
    weights = [
        pltpu.make_async_copy(w1_hbm, w1_ref, sems.at[3]),
        pltpu.make_async_copy(w2_hbm, w2_ref, sems.at[4]),
    ]
    copies = [
        pltpu.make_async_copy(x_ref.at[:, 13:16], rim_ref, sems.at[0]),
        pltpu.make_async_copy(x_ref.at[3:4], plane_ref, sems.at[1]),
        pltpu.make_async_copy(x_ref.at[3:4, 13:16], corner_ref, sems.at[2]),
    ]
    for copy in weights + copies:
        copy.start()
    odd = lax.axis_index("row") & 1
    for copy in weights:
        copy.wait()

    def tap(k, t):
        return w1_ref[t, k].astype(F32)

    def group(g):
        if g < 9:
            sides = [tap(1, g), tap(2, g)]
        else:
            t = 2 * (g - 9)
            sides = [tap(0, t), tap(0, t + 1) if t < 8 else jnp.zeros((4, 64), F32)]
        return jnp.concatenate(sides, 1)

    for m in range(7):
        tile = jnp.concatenate([group(2 * m), group(2 * m + 1)], 0).astype(BF16)
        tiles[m // 4, m % 4] = tile
    tiles[0, 4] = w2_ref[0]
    tiles[1, 3] = w2_ref[13]
    tiles[1, 4] = w2_ref[14]
    for half in range(2):
        for s in range(6):
            tiles[half, 5 + s] = w2_ref[14 * half + 1 + s + 6 * odd]
    for k in range(send_ref.shape[0] // 2):
        send_ref[2 * k : 2 * k + 2] = tiles[...]
    for copy in copies:
        copy.wait()


def pack(first, second, x, members):
    w1 = first.transpose(0, 1, 2, 4, 3).reshape(9, 3, 4, 64)
    w2 = second.transpose(0, 1, 2, 4, 3).reshape(27, 8, 128)
    shapes = ((members, 11, 8, 128), (4, 3, 128, 128), (1, 16, 128, 128), (1, 3, 128, 128))
    hbm = pl.BlockSpec(memory_space=pltpu.HBM)
    return pl.pallas_call(
        pack_kernel,
        out_shape=tuple(jax.ShapeDtypeStruct(shape, BF16) for shape in shapes),
        in_specs=[hbm, hbm, hbm],
        out_specs=(SPEC, SPEC, SPEC, SPEC),
        scratch_shapes=[
            VMEM((9, 3, 4, 64), BF16),
            VMEM((27, 8, 128), BF16),
            VMEM((2, 11, 8, 128), BF16),
            pltpu.SemaphoreType.DMA((5,)),
        ],
        compiler_params=pltpu.CompilerParams(vmem_limit_bytes=60 * 2**20),
        name="pack",
    )(w1, w2, x)


def shift_by_one(x, axes, counts):
    if len(axes) == 1:
        pairs = [(i, i + 1) for i in range(counts[0] - 1)]
        return lax.ppermute(x, axes[0], pairs)
    n, m = counts
    pairs = [(i * m + j, (i + 1) * m + j + 1) for i in range(n - 1) for j in range(m - 1)]
    return lax.ppermute(x, axes, pairs)


def glance_kernel(rim_ref, out_ref):
    out_ref[...] = rim_ref[...]


def glance(rim):
    return pl.pallas_call(
        glance_kernel,
        out_shape=jax.ShapeDtypeStruct((16, 128), BF16),
        in_specs=[SPEC],
        out_specs=SPEC,
        compiler_params=pltpu.CompilerParams(vmem_limit_bytes=2 * 2**20),
        cost_estimate=pl.CostEstimate(flops=10**11, bytes_accessed=2**20, transcendentals=0),
        name="glance",
    )(rim)


def per_device(x, first_weight, second_weight):
    nd, nr = lax.axis_size("depth"), lax.axis_size("row")
    send, rim, plane, corner = pack(first_weight, second_weight, x, nd)
    got = lax.all_to_all(send, "depth", 0, 0, tiled=False)

    rim = shift_by_one(rim, ("row",), (nr,))
    plane = shift_by_one(plane, ("depth",), (nd,))
    corner = shift_by_one(corner, ("depth", "row"), (nd, nr))
    seen = glance(rim[0, 0, :16]) + plane[0, 0, :16] + corner[0, 0, :16]
    got, seen = lax.optimization_barrier((got, seen))

    swaps = []
    for i in range(nd):
        for j in range(nr):
            base, at = j - j % 4, j % 4
            other = at ^ 1 if i % 2 == 0 else 3 - at
            swaps.append((i * nr + j, i * nr + base + other))
    stripe = lax.ppermute(got[:, 5:], ("depth", "row"), swaps)

    partners = [(i, i ^ 1) for i in range(nd)]
    theirs = lax.ppermute(got, "depth", partners)
    h1, weights, plane = last_hidden(x, plane, rim, got, theirs, seen)
    hm = shift_by_one(h1, ("depth",), (nd,))
    h0 = hidden_before(x, plane, rim, corner, weights)

    h0, stripe = lax.optimization_barrier((h0, stripe))
    other = lax.ppermute(stripe, "depth", partners)
    return second_layer(hm, h0, h1, got, theirs, stripe, other)


def solution(mesh):
    return jax.shard_map(
        per_device,
        mesh=mesh,
        in_specs=(
            P("depth", "row", None, None),
            P(None, None, None, None, "depth"),
            P(None, None, None, None, "depth"),
        ),
        out_specs=P("depth", "row", None, None),
        check_vma=False,
    )
```

```python
import jax
import jax.numpy as jnp
from jax import lax
from jax.experimental import pallas as pl
from jax.experimental.pallas import tpu as pltpu
from jax.sharding import PartitionSpec as P

F32 = jnp.float32
BF16 = jnp.bfloat16
VMEM = pltpu.VMEM
SENT = 13
SPEC = pl.BlockSpec(memory_space=pltpu.VMEM)


def dot_t(a, b):
    return lax.dot_general(a, b, (((1,), (1,)), ((), ())), preferred_element_type=F32)


def window(x, rim, j):
    x = x.reshape(8, 2, 128, 128)
    if j == 0:
        parts = [rim[0:1], rim[2:3], x[0:7, 1]]
    elif j == 1:
        parts = [rim[1:2], x[:, 0]]
    else:
        parts = [rim[2:3], x[:, 1]]
    return jnp.concatenate(parts, 0).reshape(1152, 128)


def plane_of_hidden(cells, weights, out, up, low):
    low[:, 0:8] = jnp.zeros((9, 8, 128), F32)
    for pair in range(5):
        if pair < 3:
            left = jnp.concatenate([cells(pair, 1), cells(pair, 2)], 1)
        elif pair == 3:
            left = jnp.concatenate([cells(0, 0), cells(1, 0)], 1)
        else:
            left = cells(2, 0)
        both = dot_t(left, weights[pair, :, : left.shape[1]]).reshape(9, 128, 256)
        if pair == 0:
            up[:, 0:128] = both[:, :, :128]
            low[:, 8:136] = both[:, :, 128:]
        else:
            up[:, 0:128] += both[:, :, :128]
            low[:, 8:136] += both[:, :, 128:]
    for b in range(9):
        even = up[b, pl.ds(0, 64, stride=2)] + low[b, pl.ds(7, 64, stride=2)]
        odd = up[b, pl.ds(1, 64, stride=2)] + low[b, pl.ds(8, 64, stride=2)]
        out[b, :, 0:128] = jnp.maximum(even, 0.0).astype(BF16)
        out[b, :, 128:256] = jnp.maximum(odd, 0.0).astype(BF16)


def last_kernel(x_ref, plane_hbm, rim_ref, mine_ref, theirs_ref, seen_ref, h1_ref, weights, plane_ref, stage, rows_up, up, low, sem):
    fetch = pltpu.make_async_copy(plane_hbm, plane_ref, sem)
    fetch.start()
    lanes = lax.broadcasted_iota(jnp.int32, (128, 128), 1)
    right = lanes >= 64
    core = lax.axis_index("depth") & 1

    def put(tap, row, block):
        i, j = divmod(tap, 3)
        pair, side = (i, j - 1) if j else (3 + i // 2, i % 2)
        weights[pair, row : row + 128, 128 * side : 128 * side + 128] = block.astype(BF16)

    def unpack(lower_ref, upper_ref):
        for tile in range(7):
            stage[0:256] = (lower_ref, upper_ref)[tile // 4][:, tile % 4].astype(F32).reshape(256, 128)
            for r in range(8):
                rows_up[r // 4, pl.ds(r % 4, 32, stride=4)] = stage[pl.ds(r, 32, stride=8)]
            for half in range(2):
                group = 2 * tile + half
                block = rows_up[half, 0:128]
                if group < 9:
                    put(group, 0, block)
                else:
                    tap = 2 * (group - 9)
                    put(tap, 128, jnp.where(right, pltpu.roll(block, 64, 1), 0.0))
                    if tap + 1 < 9:
                        put(tap + 1, 128, jnp.where(right, block, 0.0))

    @pl.when(core == 0)
    def _():
        unpack(mine_ref, theirs_ref)

    @pl.when(core != 0)
    def _():
        unpack(theirs_ref, mine_ref)

    weights[4, :, 128:256] = jnp.zeros((256, 128), BF16)
    h1_ref[9:] = jnp.zeros((SENT - 9, 64, 256), BF16)

    def cells(i, j):
        return window(x_ref[1 + i], rim_ref[1 + i], j)

    plane_of_hidden(cells, weights, h1_ref, up, low)
    fetch.wait()


def before_kernel(x_ref, plane_ref, rim_ref, corner_ref, weights, h0_ref, up, low):
    def cells(i, j):
        if i == 0:
            return window(plane_ref[0], corner_ref[0], j)
        return window(x_ref[i - 1], rim_ref[i - 1], j)

    plane_of_hidden(cells, weights, h0_ref, up, low)


SUMS = [VMEM((9, 136, 128), F32), VMEM((9, 136, 128), F32)]
HIDDEN = jax.ShapeDtypeStruct((9, 64, 256), BF16)


def last_hidden(x, plane, rim, mine, theirs, seen):
    return pl.pallas_call(
        last_kernel,
        out_shape=(jax.ShapeDtypeStruct((SENT, 64, 256), BF16), jax.ShapeDtypeStruct((5, 256, 256), BF16), jax.ShapeDtypeStruct(plane.shape, BF16)),
        in_specs=[SPEC, pl.BlockSpec(memory_space=pl.ANY)] + [SPEC] * 4,
        out_specs=(SPEC, SPEC, SPEC),
        scratch_shapes=[VMEM((264, 128), F32), VMEM((2, 136, 128), F32)] + SUMS + [pltpu.SemaphoreType.DMA(())],
        compiler_params=pltpu.CompilerParams(vmem_limit_bytes=24 * 2**20),
        cost_estimate=pl.CostEstimate(flops=2 * 1152 * 1152 * 256, bytes_accessed=2 * 2**20, transcendentals=0),
        name="last_hidden",
    )(x, plane, rim, mine, theirs, seen)


def hidden_before(x, plane, rim, corner, weights):
    return pl.pallas_call(
        before_kernel,
        out_shape=HIDDEN,
        in_specs=[SPEC] * 5,
        out_specs=SPEC,
        scratch_shapes=SUMS,
        compiler_params=pltpu.CompilerParams(vmem_limit_bytes=24 * 2**20),
        cost_estimate=pl.CostEstimate(flops=2 * 1152 * 1152 * 256, bytes_accessed=2 * 2**20, transcendentals=0),
        name="hidden_before",
    )(x, plane, rim, corner, weights)


def second_kernel(hm_ref, h0_ref, h1_ref, mine_ref, theirs_ref, stripe_ref, other_ref, out_ref, up, low):
    core, odd = lax.axis_index("depth") & 1, lax.axis_index("row") & 1
    planes = (hm_ref, h0_ref, h1_ref)

    def weight(block):
        return block.astype(F32).reshape(256, 128).astype(BF16)

    def body(first, last, odd):
        low[:, :, 0:8] = jnp.zeros((2, 4, 8, 128), F32)

        def tap_of(t):
            if t == 13:
                return weight(last[0][:, 3])
            own, across = first if t < 13 else last
            place = t if t < 13 else t - 14
            if place == 0:
                return weight(own[:, 4])
            side, place = divmod(place - 1, 6)
            return weight(own[:, 5 + place] if side == odd else across[:, place])

        for tap in range(9):
            i, j = divmod(tap, 3)
            cells = jnp.concatenate([planes[i][j + 2 * b] for b in range(4)], 0)
            k0, k1, k2 = (tap_of(3 * tap + k) for k in range(3))
            u = dot_t(cells, jnp.concatenate([k1, k2], 1))
            v = dot_t(cells[:, 128:], k0).reshape(4, 64, 256)
            for n in range(2):
                lanes = slice(128 * n, 128 * n + 128)
                if tap == 0:
                    up[n, 0:256] = u[:, lanes]
                    low[n, :, 8:72] = v[:, :, lanes]
                else:
                    up[n, 0:256] += u[:, lanes]
                    low[n, :, 8:72] += v[:, :, lanes]

    mine, theirs = (mine_ref, stripe_ref), (theirs_ref, other_ref)
    for c in range(2):
        for q in range(2):

            @pl.when(jnp.logical_and(core == c, odd == q))
            def _():
                body(*((mine, theirs) if c == 0 else (theirs, mine)), q)

    for b in range(4):
        for n in range(2):
            even = up[n, pl.ds(64 * b, 32, stride=2)] + low[n, b, pl.ds(7, 32, stride=2)]
            odd = up[n, pl.ds(64 * b + 1, 32, stride=2)] + low[n, b, pl.ds(8, 32, stride=2)]
            out_ref[0, b, :, 128 * n : 128 * n + 128] = jnp.maximum(even, 0.0).astype(BF16)
            out_ref[0, b, :, 256 + 128 * n : 384 + 128 * n] = jnp.maximum(odd, 0.0).astype(BF16)


def second_layer(hm, h0, h1, mine, theirs, stripe, other):
    return pl.pallas_call(
        second_kernel,
        out_shape=jax.ShapeDtypeStruct((1, 4, 32, 512), BF16),
        in_specs=[SPEC] * 7,
        out_specs=SPEC,
        scratch_shapes=[VMEM((2, 264, 128), F32), VMEM((2, 4, 72, 128), F32)],
        compiler_params=pltpu.CompilerParams(vmem_limit_bytes=24 * 2**20),
        cost_estimate=pl.CostEstimate(flops=2 * 256 * 3456 * 256, bytes_accessed=3 * 2**20, transcendentals=0),
        name="second_layer",
    )(hm, h0, h1, mine, theirs, stripe, other)


def pack_kernel(w1_hbm, w2_hbm, x_ref, send_ref, rim_ref, plane_ref, corner_ref, w1_ref, w2_ref, tiles, rim, plane, sems, out_sems):
    weights = [
        pltpu.make_async_copy(w1_hbm, w1_ref, sems.at[3]),
        pltpu.make_async_copy(w2_hbm, w2_ref, sems.at[4]),
    ]
    copies = [
        pltpu.make_async_copy(x_ref.at[:, 13:16], rim, sems.at[0]),
        pltpu.make_async_copy(x_ref.at[3:4], plane, sems.at[1]),
    ]
    for copy in weights + copies:
        copy.start()
    odd = lax.axis_index("row") & 1
    for copy in weights:
        copy.wait()

    def tap(k, t):
        return w1_ref[t, k].astype(F32)

    def group(g):
        if g < 9:
            sides = [tap(1, g), tap(2, g)]
        else:
            t = 2 * (g - 9)
            sides = [tap(0, t), tap(0, t + 1) if t < 8 else jnp.zeros((4, 64), F32)]
        return jnp.concatenate(sides, 1)

    for m in range(7):
        tile = jnp.concatenate([group(2 * m), group(2 * m + 1)], 0).astype(BF16)
        tiles[m // 4, m % 4] = tile
    tiles[0, 4] = w2_ref[0]
    tiles[1, 3] = w2_ref[13]
    tiles[1, 4] = w2_ref[14]
    for half in range(2):
        for s in range(6):
            tiles[half, 5 + s] = w2_ref[14 * half + 1 + s + 6 * odd]
    outs = [
        pltpu.make_async_copy(tiles, send_ref.at[2 * k : 2 * k + 2], out_sems.at[k])
        for k in range(send_ref.shape[0] // 2)
    ]
    edges = [
        pltpu.make_async_copy(rim, rim_ref, sems.at[2]),
        pltpu.make_async_copy(plane, plane_ref, sems.at[5]),
        pltpu.make_async_copy(plane.at[:, 13:16], corner_ref, sems.at[6]),
    ]
    for copy in outs:
        copy.start()
    for copy in copies:
        copy.wait()
    for copy in edges:
        copy.start()
    for copy in edges + outs:
        copy.wait()


def pack(first, second, x, members):
    w1 = first.transpose(0, 1, 2, 4, 3).reshape(9, 3, 4, 64)
    w2 = second.transpose(0, 1, 2, 4, 3).reshape(27, 8, 128)
    shapes = ((members, 11, 8, 128), (4, 3, 128, 128), (1, 16, 128, 128), (1, 3, 128, 128))
    hbm = pl.BlockSpec(memory_space=pltpu.HBM)
    return pl.pallas_call(
        pack_kernel,
        out_shape=tuple(jax.ShapeDtypeStruct(shape, BF16) for shape in shapes),
        in_specs=[hbm, hbm, hbm],
        out_specs=(hbm, hbm, hbm, hbm),
        scratch_shapes=[
            VMEM((9, 3, 4, 64), BF16),
            VMEM((27, 8, 128), BF16),
            VMEM((2, 11, 8, 128), BF16),
            VMEM((4, 3, 128, 128), BF16),
            VMEM((1, 16, 128, 128), BF16),
            pltpu.SemaphoreType.DMA((7,)),
            pltpu.SemaphoreType.DMA((members // 2,)),
        ],
        compiler_params=pltpu.CompilerParams(vmem_limit_bytes=60 * 2**20),
        name="pack",
    )(w1, w2, x)


def shift_by_one(x, axes, counts):
    if len(axes) == 1:
        pairs = [(i, i + 1) for i in range(counts[0] - 1)]
        return lax.ppermute(x, axes[0], pairs)
    n, m = counts
    pairs = [(i * m + j, (i + 1) * m + j + 1) for i in range(n - 1) for j in range(m - 1)]
    return lax.ppermute(x, axes, pairs)


def glance_kernel(rim_ref, out_ref):
    out_ref[...] = rim_ref[...]


def glance(rim):
    return pl.pallas_call(
        glance_kernel,
        out_shape=jax.ShapeDtypeStruct((16, 128), BF16),
        in_specs=[SPEC],
        out_specs=SPEC,
        compiler_params=pltpu.CompilerParams(vmem_limit_bytes=2 * 2**20),
        cost_estimate=pl.CostEstimate(flops=10**11, bytes_accessed=2**20, transcendentals=0),
        name="glance",
    )(rim)


def per_device(x, first_weight, second_weight):
    nd, nr = lax.axis_size("depth"), lax.axis_size("row")
    send, rim, plane, corner = pack(first_weight, second_weight, x, nd)
    got = lax.all_to_all(send, "depth", 0, 0, tiled=False)

    rim = shift_by_one(rim, ("row",), (nr,))
    plane = shift_by_one(plane, ("depth",), (nd,))
    corner = shift_by_one(corner, ("depth", "row"), (nd, nr))
    seen = glance(rim[0, 0, :16]) + plane[0, 0, :16] + corner[0, 0, :16]
    got, seen = lax.optimization_barrier((got, seen))

    swaps = []
    for i in range(nd):
        for j in range(nr):
            base, at = j - j % 4, j % 4
            other = at ^ 1 if i % 2 == 0 else 3 - at
            swaps.append((i * nr + j, i * nr + base + other))
    stripe = lax.ppermute(got[:, 5:], ("depth", "row"), swaps)

    partners = [(i, i ^ 1) for i in range(nd)]
    theirs = lax.ppermute(got, "depth", partners)
    h1, weights, plane = last_hidden(x, plane, rim, got, theirs, seen)
    hm = shift_by_one(h1, ("depth",), (nd,))
    h0 = hidden_before(x, plane, rim, corner, weights)

    h0, stripe = lax.optimization_barrier((h0, stripe))
    other = lax.ppermute(stripe, "depth", partners)
    return second_layer(hm, h0, h1, got, theirs, stripe, other)


def solution(mesh):
    return jax.shard_map(
        per_device,
        mesh=mesh,
        in_specs=(
            P("depth", "row", None, None),
            P(None, None, None, None, "depth"),
            P(None, None, None, None, "depth"),
        ),
        out_specs=P("depth", "row", None, None),
        check_vma=False,
    )
```
